512 devices in a mesh: freq: 8 (over z_lo, core), slab: 64 (over z_hi, x, y).
Axes of the slice: x: 4, y: 4, z: 16 (z_hi: 4, z_lo: 4; z = z_hi * 4 + z_lo), core: 2. Of those that a mesh axis runs over, the one named last changes fastest.
Arguments:
- source: float32 [8, 2, 64, 192, 256], P('freq', None, 'slab'), may hold values from -6 to 6
- labels: int32 [64, 192, 256], P('slab'), may hold values from 0 to 7
- speed_table: float32 [8], replicated, may hold values from 0.97 to 1.03
- atten_table: float32 [8], replicated, may hold values from 0 to 0.03
- offsets: int32 [2], replicated, may hold values from 0 to 128, as said below
Outputs:
- traces: float32 [64, 64, 32, 128], P('freq', 'slab')
The draws below stay inside these ranges and needn't reach their ends.
Inputs may be any that keep to these rules, and one draw needn't show every extreme that they name: One of the two offsets equals min(160, 128).
All inputs are finite; a program needn't handle non-finite values.
Results may differ from the reference program's by a relative error of at most 0.00012.
Values sent between devices are 32-bit elements; how exact they have to be, the bound alone decides.
A program may use at most 64 MiB of HBM per device.

```python
import math
import jax
import jax.numpy as jnp
from jax import lax

NX = 192
NY = 256
NMAT = 8
ITERS = 2
TS = 64
FX = 32
FY = 128
NF = 8
NZ = 64


def draw_offsets(key, part):
    key = jax.random.fold_in(key, 11)
    key_offset, key_order = jax.random.split(key)
    ceiling = min(NX - FX, NY - FY)
    random_offset = jax.random.randint(key_offset, (), 0, ceiling + 1)
    swapped = jax.random.randint(key_order, (), 0, 2)
    ceiling_value = jnp.int32(ceiling) + 0 * random_offset
    return jnp.where(swapped == 1, jnp.stack([ceiling_value, random_offset]), jnp.stack([random_offset, ceiling_value])).astype(jnp.int32)


def with_ends(drawn, own_key, low, largest):
    spot = [jax.random.randint(jax.random.fold_in(own_key, axis), (), 0, length) for axis, length in enumerate(drawn.shape)]
    longest = drawn.shape.index(max(drawn.shape))
    beside = spot[:longest] + [(spot[longest] + 1) % drawn.shape[longest]] + spot[longest + 1:]
    return drawn.at[tuple(spot)].set(low).at[tuple(beside)].set(largest)


def steps_of(rng, shape, cuts, low, top_value):
    gain, own = 1.0, jax.random.fold_in(rng, 6)
    for position, blocks in cuts:
        steps = jnp.exp(jax.random.uniform(jax.random.fold_in(own, position), (blocks,), jnp.float32, low / len(cuts), top_value / len(cuts)))
        gain = gain * jnp.repeat(steps, shape[position] // blocks).reshape([-1 if axis == position else 1 for axis in range(len(shape))])
    return gain


def centred(rng, extent, spread, most, cuts=(), kind=jnp.bfloat16):
    values = spread * jax.random.normal(rng, extent, jnp.float32)
    if cuts:
        values = values * steps_of(rng, extent, cuts, -0.22, 0.18)
    return jnp.clip(values, -most, most).astype(kind)


def setup_inputs(seed: int = 0) -> dict:
    splits = jax.random.split(jax.random.key(seed), 6)
    source = centred(splits[0], (NF, 2, NZ, NX, NY), 1.0, 6.0, ((0, 8), (2, 64)), jnp.float32)
    labels = with_ends(jax.random.randint(splits[1], (NZ, NX, NY), 0, NMAT), jax.random.fold_in(splits[1], 1), 0, NMAT - 1).astype(jnp.int32)
    speed_table = jnp.clip(jnp.exp(jax.random.uniform(splits[2], (NMAT,), jnp.float32, math.log(0.97), math.log(1.03))), 0.97, 1.03)
    atten_table = jnp.clip(jax.random.uniform(splits[3], (NMAT,), jnp.float32, 0.0, 0.03), 0.0, 0.03)
    offsets = draw_offsets(jax.random.fold_in(splits[5], 71), 0)
    return dict(source=source, labels=labels, speed_table=speed_table, atten_table=atten_table, offsets=offsets)


base_bin = 4
k_unit = 0.1

def squared_wave(count):
    return (2.0 * math.pi * jnp.fft.fftfreq(count).astype(jnp.float32)) ** 2

def reference(source, labels, speed_table, atten_table, offsets):
    speed_cell = speed_table[labels]
    atten_cell = atten_table[labels]
    psq = squared_wave(NZ)[:, None, None] + squared_wave(NX)[None, :, None] + squared_wave(NY)[None, None, :]
    times = jnp.arange(TS, dtype=jnp.int32)
    traces = jnp.zeros((TS, NZ, FX, FY), jnp.float32)
    for frequency in range(NF):
        wave = k_unit * (base_bin + frequency)
        k0sq = wave * wave
        table_sq = (wave / speed_table) ** 2
        table_real = table_sq * (1.0 - atten_table ** 2)
        table_imag = 2.0 * table_sq * atten_table
        epsilon = jnp.max(jnp.sqrt((table_real - k0sq) ** 2 + table_imag ** 2)) + 0.1 * k0sq
        cell_sq = (wave / speed_cell) ** 2
        potential = lax.complex(cell_sq * (1.0 - atten_cell ** 2) - k0sq, 2.0 * cell_sq * atten_cell - epsilon)
        gamma_cell = lax.complex(-jnp.imag(potential) / epsilon, jnp.real(potential) / epsilon)
        shifted = psq - k0sq
        denom = shifted * shifted + epsilon * epsilon
        green = lax.complex(shifted / denom, epsilon / denom + 0.0 * shifted)
        drive = lax.complex(source[frequency, 0], source[frequency, 1])
        field = jnp.zeros_like(drive)
        for iteration in range(ITERS):
            work_field = potential * field + drive
            filtered = jnp.fft.ifftn(green * jnp.fft.fftn(work_field))
            field = field - gamma_cell * (field - filtered)
        focal = lax.dynamic_slice(field, (jnp.int32(0), offsets[0].astype(jnp.int32), offsets[1].astype(jnp.int32)), (NZ, FX, FY))
        phase_index = times * (base_bin + frequency) % TS
        angle = phase_index.astype(jnp.float32) * (2.0 * math.pi / TS)
        traces = traces + jnp.cos(angle)[:, None, None, None] * jnp.real(focal)[None] - jnp.sin(angle)[:, None, None, None] * jnp.imag(focal)[None]
    return traces
```

```python
import functools
import math

import jax
import jax.numpy as jnp
import numpy as np
from jax import lax
from jax.experimental import pallas as pl
from jax.experimental.pallas import tpu as pltpu
from jax.sharding import PartitionSpec as P

MESH = pl.DeviceIdType.MESH
NX, NY, NZ = 192, 256, 64
FX, FY, NF, TS, NMAT = 32, 128, 8, 64, 8
BASE_BIN, K_UNIT = 4, 0.1
F32, BF16 = jnp.float32, jnp.bfloat16


def dft_tables(count):
    points = np.arange(count)
    angle = (points[:, None] * points[None, :] % count) * (2.0 * math.pi / count)
    return np.cos(angle), np.sin(angle)


def halves(table):
    high = np.asarray(table, np.float32).astype(jnp.bfloat16)
    low = (np.asarray(table, np.float64) - high.astype(np.float64)).astype(jnp.bfloat16)
    return high, low


def constant_tables():
    cos_y, sin_y = dft_tables(NY)
    high, low = halves(np.concatenate([cos_y, sin_y], 1))
    table_y = np.concatenate([high, high, low], 0)
    cos_x, sin_x = dft_tables(NX)
    high, low = halves(np.concatenate([cos_x, sin_x], 0))
    table_x = np.concatenate([high, high, low], 1)
    cos_z, sin_z = dft_tables(NZ)
    high, low = halves(np.concatenate([cos_z, sin_z], 0))
    table_z = np.concatenate([high, high, low], 1)
    angle = np.arange(TS) * (2.0 * math.pi / TS)
    wave = np.stack([np.cos(angle), np.sin(angle)]).astype(np.float32)
    return table_y, table_x, table_z, wave


def split(value):
    high = value.astype(BF16)
    return high, (value - high.astype(F32)).astype(BF16)


def dot(left, right):
    return jnp.dot(left, right, preferred_element_type=F32)


def times_table(value, table):
    high, low = split(value)
    return dot(jnp.concatenate([high, low, high], 1), table)


def table_times(table, value):
    high, low = split(value)
    return dot(table, jnp.concatenate([high, low, high], 0))


def combine_rows(product, rows, width, sign):
    real = product[:rows, :width] - sign * product[rows:, width:]
    imag = product[rows:, :width] + sign * product[:rows, width:]
    return real, imag


def combine_tables(product, rows, width, sign):
    real = product[:rows, :width] - sign * product[rows:, width:]
    imag = product[:rows, width:] + sign * product[rows:, :width]
    return real, imag


def along_y(real, imag, table, sign):
    rows = real.shape[0]
    return combine_rows(
        times_table(jnp.concatenate([real, imag], 0), table), rows, NY, sign
    )


def along_x(real, imag, table, sign):
    width = real.shape[1]
    return combine_tables(
        table_times(table, jnp.concatenate([real, imag], 1)), NX, width, sign
    )


def along_z(real, imag, table, sign):
    width = real.shape[1]
    return combine_tables(
        table_times(table, jnp.concatenate([real, imag], 1)), NZ, width, sign
    )


def put_rows(ref, real, imag):
    for part, value in enumerate((real, imag)):
        for i in range(3):
            for half in range(2):
                ref[pl.ds(4 * i + 2 * part + half, 64, stride=12), :] = value[
                    64 * i : 64 * i + 64, 128 * half : 128 * half + 128
                ]


def get_rows(ref, part, per):
    return jnp.concatenate(
        [
            jnp.concatenate(
                [
                    ref[pl.ds(2 * per * i + per * part + half, 64, stride=6 * per), :]
                    for half in range(per)
                ],
                1,
            )
            for i in range(3)
        ],
        0,
    )


def get_lines(ref, part):
    return jnp.concatenate(
        [
            ref[pl.ds(4 * i + 2 * part + half, 64, stride=12), :]
            for i in range(3)
            for half in range(2)
        ],
        1,
    )


def put_lines(ref, real, imag):
    for part, value in enumerate((real, imag)):
        for i in range(3):
            for half in range(2):
                at = 256 * i + 128 * half
                ref[pl.ds(4 * i + 2 * part + half, 64, stride=12), :] = value[:, at : at + 128]


def folded_square(index, count):
    folded = jnp.where(index <= count // 2, index, index - count)
    wavenum = folded.astype(F32) * (2.0 * math.pi / count)
    return wavenum * wavenum


def role_device(frequency, k):
    return 4 * (frequency % 2) + k // 16, 16 * (frequency // 2) + k % 16


def kernel(
    source, labels, speed, atten, offsets, table_y, table_x, table_z, wave_table, out,
    send1, recv1, send2, recv2, send3, recv3, send4, recv4, tissue, window, windows,
    green, spectrum, pot_buf, field_buf, sel_y, sel_x, send_sem, recv_sem,
):
    f = lax.axis_index("freq")
    s = lax.axis_index("slab")
    freq = 2 * (s // 16) + f // 4
    mine = 16 * (f % 4) + s % 16
    home = freq == f

    barrier = pltpu.get_barrier_semaphore()

    def greet(i, carry):
        pl.semaphore_signal(barrier, inc=1, device_id=(freq, i), device_id_type=MESH)
        return carry

    lax.fori_loop(0, 64, greet, 0)

    def greet_last(i, carry):
        pl.semaphore_signal(barrier, inc=1, device_id=role_device(i, s), device_id_type=MESH)
        return carry

    lax.fori_loop(0, NF, greet_last, 0)

    def remote(src, dst, sem, device):
        return pltpu.make_async_remote_copy(
            src_ref=src,
            dst_ref=dst,
            send_sem=send_sem.at[sem],
            recv_sem=recv_sem.at[sem],
            device_id=device,
            device_id_type=MESH,
        )

    def exchange(src, dst, rows, sem):
        def step(i, carry):
            k = lax.rem(mine + i, 64)
            remote(
                src.at[pl.ds(rows * k, rows)],
                dst.at[pl.ds(rows * mine, rows)],
                sem,
                role_device(freq, k),
            ).start()
            return carry

        lax.fori_loop(1, 64, step, 0)
        own = pl.ds(rows * mine, rows)
        pltpu.make_async_copy(src.at[own], dst.at[own], recv_sem.at[sem]).start()

    def arrived(ref, sem):
        pltpu.make_async_copy(ref, ref, recv_sem.at[sem]).wait()

    def sent(ref, rows, sem):
        part = ref.at[pl.ds(0, rows)]
        pltpu.make_async_copy(part, part, send_sem.at[sem]).wait()

    real, imag = along_y(source[0], source[1], table_y[...], -1.0)
    real, imag = along_x(real, imag, table_x[...], -1.0)
    put_rows(send1, real, imag)
    pl.semaphore_wait(barrier, 64 + NF)

    def scatter(i, carry):
        k = lax.rem(mine + i, 64)
        remote(
            send1.at[pl.ds(12 * k, 12)],
            recv1.at[pl.ds(12 * s, 12)],
            0,
            role_device(f, k),
        ).start()
        return carry

    lax.fori_loop(1, 64, scatter, 0)
    own_send = send1.at[pl.ds(12 * mine, 12)]
    own_recv = recv1.at[pl.ds(12 * s, 12)]

    @pl.when(home)
    def _():
        pltpu.make_async_copy(own_send, own_recv, recv_sem.at[0]).start()

    @pl.when(jnp.logical_not(home))
    def _():
        remote(own_send, own_recv, 0, role_device(f, mine)).start()

    stays = home & (mine == s)

    @pl.when(stays)
    def _():
        pltpu.make_async_copy(labels, tissue, recv_sem.at[1]).start()

    @pl.when(jnp.logical_not(stays))
    def _():
        remote(labels, tissue, 1, role_device(f, s)).start()

    wave = K_UNIT * (BASE_BIN + freq).astype(F32)
    k0sq = wave * wave
    shape = (8, 128)
    pot_real, pot_imag = [], []
    largest = jnp.zeros(shape, F32)
    for m in range(NMAT):
        ratio = jnp.full(shape, wave) / jnp.full(shape, speed[m])
        ratio = ratio * ratio
        damp = jnp.full(shape, atten[m])
        pot_real.append(ratio * (1.0 - damp * damp) - k0sq)
        pot_imag.append(2.0 * ratio * damp)
        largest = jnp.maximum(largest, pot_real[m] * pot_real[m] + pot_imag[m] * pot_imag[m])
    eps = jnp.sqrt(largest) + 0.1 * k0sq
    pot_imag = [value - eps for value in pot_imag]
    eps_row = eps[0:1, 0:1]
    lines = (NZ, NY)
    z_sq = folded_square(lax.broadcasted_iota(jnp.int32, lines, 0), NZ)
    y_sq = folded_square(lax.broadcasted_iota(jnp.int32, lines, 1), NY)
    for i in range(3):
        x_sq = folded_square(jnp.full(lines, 64 * i + mine, jnp.int32), NX)
        shifted = z_sq + x_sq + y_sq - k0sq
        denom = shifted * shifted + eps_row * eps_row
        weight = (1.0 / (NX * NY * NZ)) / denom
        green[0, :, NY * i : NY * (i + 1)] = shifted * weight
        green[1, :, NY * i : NY * (i + 1)] = eps_row * weight

    off_x, off_y = offsets[0], offsets[1]
    pick_y = (
        lax.broadcasted_iota(jnp.int32, (NY, FY), 0)
        == lax.broadcasted_iota(jnp.int32, (NY, FY), 1) + off_y
    ).astype(F32).astype(BF16)
    pick_x = (
        lax.broadcasted_iota(jnp.int32, (FX, NX), 1)
        == lax.broadcasted_iota(jnp.int32, (FX, NX), 0) + off_x
    ).astype(F32).astype(BF16)
    for j, at in enumerate((0, 2 * NY)):
        for part in range(2):
            piece = table_y[at : at + NY, NY * part : NY * (part + 1)]
            sel_y[NY * j : NY * (j + 1), FY * part : FY * (part + 1)] = dot(piece, pick_y).astype(BF16)
    for part in range(2):
        piece = table_x[NX * part : NX * (part + 1), :]
        sel_x[FX * part : FX * (part + 1), :] = dot(pick_x, piece).astype(BF16)

    arrived(recv1, 0)
    real, imag = along_z(get_lines(recv1, 0), get_lines(recv1, 1), table_z[...], -1.0)
    spectrum[0] = real
    spectrum[1] = imag

    def filtered(real, imag):
        green_real, green_imag = green[0], green[1]
        return along_z(
            real * green_real - imag * green_imag,
            real * green_imag + imag * green_real,
            table_z[...],
            1.0,
        )

    real, imag = filtered(real, imag)
    put_lines(send2, real, imag)
    exchange(send2, recv2, 12, 2)

    arrived(tissue, 1)
    plane = (NX, NY)
    ids = tissue[...]
    cell_real = jnp.zeros(plane, F32)
    cell_imag = jnp.zeros(plane, F32)
    for m in range(NMAT):
        matched = ids == m
        cell_real = jnp.where(matched, pot_real[m][0:1, 0:1], cell_real)
        cell_imag = jnp.where(matched, pot_imag[m][0:1, 0:1], cell_imag)
    pot_buf[0] = cell_real
    pot_buf[1] = cell_imag

    arrived(recv2, 2)
    real, imag = along_x(get_rows(recv2, 0, 2), get_rows(recv2, 1, 2), table_x[...], 1.0)
    real, imag = along_y(real, imag, table_y[...], 1.0)
    cell_real, cell_imag = pot_buf[0], pot_buf[1]
    inv_eps = 1.0 / eps_row
    gamma_real, gamma_imag = -cell_imag * inv_eps, cell_real * inv_eps
    field_real = gamma_real * real - gamma_imag * imag
    field_imag = gamma_real * imag + gamma_imag * real
    field_buf[0] = field_real
    field_buf[1] = field_imag
    work_real = cell_real * field_real - cell_imag * field_imag
    work_imag = cell_real * field_imag + cell_imag * field_real
    real, imag = along_y(work_real, work_imag, table_y[...], -1.0)
    real, imag = along_x(real, imag, table_x[...], -1.0)
    put_rows(send3, real, imag)
    exchange(send3, recv3, 12, 3)

    def focal(high_mid_low):
        total = None
        for piece in high_mid_low:
            picked = dot(dot(pick_x, piece).astype(BF16), pick_y)
            total = picked if total is None else total + picked
        return total

    def thirds(value):
        high, rest = split(value)
        low = (value - high.astype(F32) - rest.astype(F32)).astype(BF16)
        return high, rest, low

    focal_ids = focal([tissue[...].astype(F32).astype(BF16)])
    focal_real = focal(thirds(field_buf[0]))
    focal_imag = focal(thirds(field_buf[1]))
    cell_real = jnp.zeros((FX, FY), F32)
    cell_imag = jnp.zeros((FX, FY), F32)
    for m in range(NMAT):
        matched = focal_ids == float(m)
        cell_real = jnp.where(matched, pot_real[m][0:1, 0:1], cell_real)
        cell_imag = jnp.where(matched, pot_imag[m][0:1, 0:1], cell_imag)
    gamma_real, gamma_imag = -cell_imag * inv_eps, cell_real * inv_eps

    arrived(recv3, 3)
    real, imag = along_z(get_lines(recv3, 0), get_lines(recv3, 1), table_z[...], -1.0)
    real, imag = filtered(real + spectrum[0], imag + spectrum[1])
    stacked = jnp.concatenate(
        [value[:, NY * i : NY * (i + 1)] for value in (real, imag) for i in range(3)], 0
    )
    high, low = split(stacked)
    product = dot(jnp.concatenate([high, low], 1), jnp.concatenate([sel_y[:NY], sel_y[:NY]], 0)) + dot(
        high, sel_y[NY:]
    )
    real, imag = combine_rows(product, 3 * NZ, FY, 1.0)
    for part, value in enumerate((real, imag)):
        for i in range(3):
            send4[pl.ds(2 * i + part, 64, stride=6), :] = value[64 * i : 64 * i + 64]
    exchange(send4, recv4, 6, 4)
    arrived(recv4, 4)
    product = table_times(
        sel_x[...], jnp.concatenate([get_rows(recv4, 0, 1), get_rows(recv4, 1, 1)], 1)
    )
    real, imag = combine_tables(product, FX, FY, 1.0)
    diff_real = focal_real - real
    diff_imag = focal_imag - imag
    window[:FX] = focal_real - (gamma_real * diff_real - gamma_imag * diff_imag)
    window[FX:] = focal_imag - (gamma_real * diff_imag + gamma_imag * diff_real)

    here = mine == s

    def hand_out(i, carry):
        target = lax.rem(f + i, NF)

        @pl.when(here & (i == 0))
        def _():
            pltpu.make_async_copy(window, windows.at[freq], recv_sem.at[5]).start()

        @pl.when(jnp.logical_not(here & (i == 0)))
        def _():
            remote(window, windows.at[freq], 5, (target, mine)).start()

        return carry

    lax.fori_loop(0, NF, hand_out, 0)
    arrived(windows, 5)
    for t in range(8):
        total = jnp.zeros((FX, FY), F32)
        for j in range(NF):
            phase = (8 * f + t) * (BASE_BIN + j) % TS
            total = total + wave_table[0, phase] * windows[j, :FX] - wave_table[1, phase] * windows[j, FX:]
        out[t, 0] = total

    @pl.when(home)
    def _():
        sent(send1, 12 * 63, 0)

    @pl.when(jnp.logical_not(home))
    def _():
        sent(send1, 12 * 64, 0)

    @pl.when(jnp.logical_not(stays))
    def _():
        pltpu.make_async_copy(labels, labels, send_sem.at[1]).wait()

    sent(send2, 12 * 63, 2)
    sent(send3, 12 * 63, 3)
    sent(send4, 6 * 63, 4)

    @pl.when(here)
    def _():
        part = windows.at[pl.ds(0, NF - 1)]
        pltpu.make_async_copy(part, part, send_sem.at[5]).wait()

    @pl.when(jnp.logical_not(here))
    def _():
        pltpu.make_async_copy(windows, windows, send_sem.at[5]).wait()


def solution(mesh):
    table_y, table_x, table_z, wave_table = constant_tables()
    vmem = pl.BlockSpec(memory_space=pltpu.VMEM)
    smem = pl.BlockSpec(memory_space=pltpu.SMEM)

    def local(source, labels, speed_table, atten_table, offsets):
        chunks = pltpu.VMEM((64 * 12, 128), F32)
        small = pltpu.VMEM((64 * 6, 128), F32)
        return pl.pallas_call(
            kernel,
            out_shape=jax.ShapeDtypeStruct((TS // NF, 1, FX, FY), F32),
            in_specs=[vmem, vmem, smem, smem, smem, vmem, vmem, vmem, smem],
            out_specs=vmem,
            scratch_shapes=[
                chunks, chunks, chunks, chunks, chunks, chunks, small, small,
                pltpu.VMEM((NX, NY), jnp.int32),
                pltpu.VMEM((2 * FX, FY), F32),
                pltpu.VMEM((NF, 2 * FX, FY), F32),
                pltpu.VMEM((2, NZ, 3 * NY), F32),
                pltpu.VMEM((2, NZ, 3 * NY), F32),
                pltpu.VMEM((2, NX, NY), F32),
                pltpu.VMEM((2, NX, NY), F32),
                pltpu.VMEM((2 * NY, 2 * FY), BF16),
                pltpu.VMEM((2 * FX, 3 * NX), BF16),
                pltpu.SemaphoreType.DMA((6,)),
                pltpu.SemaphoreType.DMA((6,)),
            ],
            compiler_params=pltpu.CompilerParams(
                collective_id=0, has_side_effects=True, vmem_limit_bytes=40 * 1024 * 1024
            ),
        )(
            source[0, :, 0], labels[0], speed_table, atten_table, offsets,
            jnp.asarray(table_y), jnp.asarray(table_x), jnp.asarray(table_z), jnp.asarray(wave_table),
        )

    return jax.shard_map(
        local,
        mesh=mesh,
        in_specs=(P("freq", None, "slab", None, None), P("slab", None, None), P(), P(), P()),
        out_specs=P("freq", "slab", None, None),
        check_vma=False,
    )
```

```python
import functools
import math

import jax
import jax.numpy as jnp
import numpy as np
from jax import lax
from jax.experimental import pallas as pl
from jax.experimental.pallas import tpu as pltpu
from jax.sharding import PartitionSpec as P

MESH = pl.DeviceIdType.MESH
NX, NY, NZ = 192, 256, 64
FX, FY, NF, TS, NMAT = 32, 128, 8, 64, 8
BASE_BIN, K_UNIT = 4, 0.1
F32, BF16 = jnp.float32, jnp.bfloat16


def dft_tables(count):
    points = np.arange(count)
    angle = (points[:, None] * points[None, :] % count) * (2.0 * math.pi / count)
    return np.cos(angle), np.sin(angle)


def halves(table):
    high = np.asarray(table, np.float32).astype(jnp.bfloat16)
    low = (np.asarray(table, np.float64) - high.astype(np.float64)).astype(jnp.bfloat16)
    return high, low


def constant_tables():
    cos_y, sin_y = dft_tables(NY)
    high, low = halves(np.concatenate([cos_y, sin_y], 1))
    table_y = np.concatenate([high, high, low], 0)
    cos_x, sin_x = dft_tables(NX)
    high, low = halves(np.concatenate([cos_x, sin_x], 0))
    table_x = np.concatenate([high, high, low], 1)
    cos_z, sin_z = dft_tables(NZ)
    high, low = halves(np.concatenate([cos_z, sin_z], 0))
    table_z = np.concatenate([high, high, low], 1)
    angle = np.arange(TS) * (2.0 * math.pi / TS)
    wave = np.stack([np.cos(angle), np.sin(angle)]).astype(np.float32)
    return table_y, table_x, table_z, wave


def split(value):
    high = value.astype(BF16)
    return high, (value - high.astype(F32)).astype(BF16)


def dot(left, right):
    return jnp.dot(left, right, preferred_element_type=F32)


def times_table(value, table):
    high, low = split(value)
    return dot(jnp.concatenate([high, low, high], 1), table)


def table_times(table, value):
    high, low = split(value)
    return dot(table, jnp.concatenate([high, low, high], 0))


def combine_rows(product, rows, width, sign):
    real = product[:rows, :width] - sign * product[rows:, width:]
    imag = product[rows:, :width] + sign * product[:rows, width:]
    return real, imag


def combine_tables(product, rows, width, sign):
    real = product[:rows, :width] - sign * product[rows:, width:]
    imag = product[:rows, width:] + sign * product[rows:, :width]
    return real, imag


def along_y(real, imag, table, sign):
    rows = real.shape[0]
    return combine_rows(
        times_table(jnp.concatenate([real, imag], 0), table), rows, NY, sign
    )


def along_x(real, imag, table, sign):
    width = real.shape[1]
    return combine_tables(
        table_times(table, jnp.concatenate([real, imag], 1)), NX, width, sign
    )


def along_z(real, imag, table, sign):
    width = real.shape[1]
    return combine_tables(
        table_times(table, jnp.concatenate([real, imag], 1)), NZ, width, sign
    )


def put_rows(ref, real, imag):
    for part, value in enumerate((real, imag)):
        for i in range(3):
            for half in range(2):
                ref[pl.ds(4 * i + 2 * part + half, 64, stride=12), :] = value[
                    64 * i : 64 * i + 64, 128 * half : 128 * half + 128
                ]


def get_rows(ref, part, per):
    return jnp.concatenate(
        [
            jnp.concatenate(
                [
                    ref[pl.ds(2 * per * i + per * part + half, 64, stride=6 * per), :]
                    for half in range(per)
                ],
                1,
            )
            for i in range(3)
        ],
        0,
    )


def get_lines(ref, part):
    return jnp.concatenate(
        [
            ref[pl.ds(4 * i + 2 * part + half, 64, stride=12), :]
            for i in range(3)
            for half in range(2)
        ],
        1,
    )


def put_lines(ref, real, imag):
    for part, value in enumerate((real, imag)):
        for i in range(3):
            for half in range(2):
                at = 256 * i + 128 * half
                ref[pl.ds(4 * i + 2 * part + half, 64, stride=12), :] = value[:, at : at + 128]


def folded_square(index, count):
    folded = jnp.where(index <= count // 2, index, index - count)
    wavenum = folded.astype(F32) * (2.0 * math.pi / count)
    return wavenum * wavenum


def role_device(frequency, k):
    block = frequency // 2 + 4 * (frequency % 2)
    return 4 * (block % 2) + k // 16, 16 * (block // 2) + k % 16


def kernel(
    source_in, labels, speed, atten, offsets, table_y_in, table_x_in, table_z_in, wave_table, out,
    source, table_y, table_x, table_z,
    send1, recv1, send2, recv2, send3, recv3, send4, recv4, tissue, window, windows,
    green, spectrum, field_buf, sel_y, sel_x, load_sem, send_sem, recv_sem, pass_sem, relay_sem,
):
    f = lax.axis_index("freq")
    s = lax.axis_index("slab")
    block = 2 * (s // 16) + f // 4
    freq = 2 * (block % 4) + block // 4
    mine = 16 * (f % 4) + s % 16
    home = freq == f

    loads = [
        pltpu.make_async_copy(src, dst, load_sem.at[i])
        for i, (src, dst) in enumerate(
            ((source_in, source), (table_y_in, table_y), (table_x_in, table_x), (table_z_in, table_z))
        )
    ]
    for load in loads:
        load.start()

    barrier = pltpu.get_barrier_semaphore()

    def greet(i, carry):
        pl.semaphore_signal(barrier, inc=1, device_id=(freq, i), device_id_type=MESH)
        return carry

    lax.fori_loop(0, 64, greet, 0)

    for step in range(1, NF):
        near = lax.rem(f + step, NF)
        pl.semaphore_signal(barrier, inc=1, device_id=(near, s), device_id_type=MESH)

    def remote(src, dst, sem, device):
        return pltpu.make_async_remote_copy(
            src_ref=src,
            dst_ref=dst,
            send_sem=send_sem.at[sem],
            recv_sem=recv_sem.at[sem],
            device_id=device,
            device_id_type=MESH,
        )

    def exchange(src, dst, rows, sem):
        def step(i, carry):
            k = lax.rem(mine + i, 64)
            remote(
                src.at[pl.ds(rows * k, rows)],
                dst.at[pl.ds(rows * mine, rows)],
                sem,
                role_device(freq, k),
            ).start()
            return carry

        lax.fori_loop(1, 64, step, 0)
        own = pl.ds(rows * mine, rows)
        pltpu.make_async_copy(src.at[own], dst.at[own], recv_sem.at[sem]).start()

    def arrived(ref, sem):
        pltpu.make_async_copy(ref, ref, recv_sem.at[sem]).wait()

    def sent(ref, rows, sem):
        part = ref.at[pl.ds(0, rows)]
        pltpu.make_async_copy(part, part, send_sem.at[sem]).wait()

    loads[0].wait()
    loads[1].wait()
    real, imag = along_y(source[0], source[1], table_y[...], -1.0)
    loads[2].wait()
    real, imag = along_x(real, imag, table_x[...], -1.0)
    put_rows(send1, real, imag)
    pl.semaphore_wait(barrier, 64 + NF - 1)

    def scatter(i, carry):
        k = lax.rem(mine + i, 64)
        remote(
            send1.at[pl.ds(12 * k, 12)],
            recv1.at[pl.ds(12 * s, 12)],
            0,
            role_device(f, k),
        ).start()
        return carry

    lax.fori_loop(1, 64, scatter, 0)
    own_send = send1.at[pl.ds(12 * mine, 12)]
    own_recv = recv1.at[pl.ds(12 * s, 12)]

    @pl.when(home)
    def _():
        pltpu.make_async_copy(own_send, own_recv, recv_sem.at[0]).start()

    @pl.when(jnp.logical_not(home))
    def _():
        remote(own_send, own_recv, 0, role_device(f, mine)).start()

    stays = home & (mine == s)

    wave = K_UNIT * (BASE_BIN + freq).astype(F32)
    k0sq = wave * wave
    shape = (8, 128)
    pot_real, pot_imag = [], []
    largest = jnp.zeros(shape, F32)
    for m in range(NMAT):
        ratio = jnp.full(shape, wave) / jnp.full(shape, speed[m])
        ratio = ratio * ratio
        damp = jnp.full(shape, atten[m])
        pot_real.append(ratio * (1.0 - damp * damp) - k0sq)
        pot_imag.append(2.0 * ratio * damp)
        largest = jnp.maximum(largest, pot_real[m] * pot_real[m] + pot_imag[m] * pot_imag[m])
    eps = jnp.sqrt(largest) + 0.1 * k0sq
    pot_imag = [value - eps for value in pot_imag]
    eps_row = eps[0:1, 0:1]
    lines = (NZ, NY)
    z_sq = folded_square(lax.broadcasted_iota(jnp.int32, lines, 0), NZ)
    y_sq = folded_square(lax.broadcasted_iota(jnp.int32, lines, 1), NY)
    for i in range(3):
        x_sq = folded_square(jnp.full(lines, 64 * i + mine, jnp.int32), NX)
        shifted = z_sq + x_sq + y_sq - k0sq
        denom = shifted * shifted + eps_row * eps_row
        weight = (1.0 / (NX * NY * NZ)) / denom
        green[0, :, NY * i : NY * (i + 1)] = shifted * weight
        green[1, :, NY * i : NY * (i + 1)] = eps_row * weight

    off_x, off_y = offsets[0], offsets[1]
    pick_y = (
        lax.broadcasted_iota(jnp.int32, (NY, FY), 0)
        == lax.broadcasted_iota(jnp.int32, (NY, FY), 1) + off_y
    ).astype(F32).astype(BF16)
    pick_x = (
        lax.broadcasted_iota(jnp.int32, (FX, NX), 1)
        == lax.broadcasted_iota(jnp.int32, (FX, NX), 0) + off_x
    ).astype(F32).astype(BF16)
    for j, at in enumerate((0, 2 * NY)):
        for part in range(2):
            piece = table_y[at : at + NY, NY * part : NY * (part + 1)]
            sel_y[NY * j : NY * (j + 1), FY * part : FY * (part + 1)] = dot(piece, pick_y).astype(BF16)
    for part in range(2):
        piece = table_x[NX * part : NX * (part + 1), :]
        sel_x[FX * part : FX * (part + 1), :] = dot(pick_x, piece).astype(BF16)

    loads[3].wait()
    @pl.when(home)
    def _():
        sent(send1, 12 * 63, 0)

    @pl.when(jnp.logical_not(home))
    def _():
        sent(send1, 12 * 64, 0)

    @pl.when(stays)
    def _():
        pltpu.make_async_copy(labels, tissue, recv_sem.at[1]).start()

    @pl.when(jnp.logical_not(stays))
    def _():
        remote(labels, tissue, 1, role_device(f, s)).start()

    arrived(recv1, 0)
    real, imag = along_z(get_lines(recv1, 0), get_lines(recv1, 1), table_z[...], -1.0)
    spectrum[0] = real
    spectrum[1] = imag

    def filtered(real, imag):
        green_real, green_imag = green[0], green[1]
        return along_z(
            real * green_real - imag * green_imag,
            real * green_imag + imag * green_real,
            table_z[...],
            1.0,
        )

    real, imag = filtered(real, imag)
    put_lines(send2, real, imag)
    exchange(send2, recv2, 12, 2)

    arrived(recv2, 2)
    real, imag = along_x(get_rows(recv2, 0, 2), get_rows(recv2, 1, 2), table_x[...], 1.0)
    real, imag = along_y(real, imag, table_y[...], 1.0)
    arrived(tissue, 1)
    plane = (NX, NY)
    ids = tissue[...]
    cell_real = jnp.zeros(plane, F32)
    cell_imag = jnp.zeros(plane, F32)
    for m in range(NMAT):
        matched = ids == m
        cell_real = jnp.where(matched, pot_real[m][0:1, 0:1], cell_real)
        cell_imag = jnp.where(matched, pot_imag[m][0:1, 0:1], cell_imag)
    inv_eps = 1.0 / eps_row
    gamma_real, gamma_imag = -cell_imag * inv_eps, cell_real * inv_eps
    field_real = gamma_real * real - gamma_imag * imag
    field_imag = gamma_real * imag + gamma_imag * real
    field_buf[0] = field_real
    field_buf[1] = field_imag
    work_real = cell_real * field_real - cell_imag * field_imag
    work_imag = cell_real * field_imag + cell_imag * field_real
    real, imag = along_y(work_real, work_imag, table_y[...], -1.0)
    real, imag = along_x(real, imag, table_x[...], -1.0)
    put_rows(send3, real, imag)
    exchange(send3, recv3, 12, 3)

    def focal(high_mid_low):
        total = None
        for piece in high_mid_low:
            picked = dot(dot(pick_x, piece).astype(BF16), pick_y)
            total = picked if total is None else total + picked
        return total

    def thirds(value):
        high, rest = split(value)
        low = (value - high.astype(F32) - rest.astype(F32)).astype(BF16)
        return high, rest, low

    focal_ids = focal([tissue[...].astype(F32).astype(BF16)])
    focal_real = focal(thirds(field_buf[0]))
    focal_imag = focal(thirds(field_buf[1]))
    cell_real = jnp.zeros((FX, FY), F32)
    cell_imag = jnp.zeros((FX, FY), F32)
    for m in range(NMAT):
        matched = focal_ids == float(m)
        cell_real = jnp.where(matched, pot_real[m][0:1, 0:1], cell_real)
        cell_imag = jnp.where(matched, pot_imag[m][0:1, 0:1], cell_imag)
    gamma_real, gamma_imag = -cell_imag * inv_eps, cell_real * inv_eps

    arrived(recv3, 3)
    real, imag = along_z(get_lines(recv3, 0), get_lines(recv3, 1), table_z[...], -1.0)
    real, imag = filtered(real + spectrum[0], imag + spectrum[1])
    stacked = jnp.concatenate(
        [value[:, NY * i : NY * (i + 1)] for value in (real, imag) for i in range(3)], 0
    )
    high, low = split(stacked)
    product = dot(jnp.concatenate([high, low], 1), jnp.concatenate([sel_y[:NY], sel_y[:NY]], 0)) + dot(
        high, sel_y[NY:]
    )
    real, imag = combine_rows(product, 3 * NZ, FY, 1.0)
    for part, value in enumerate((real, imag)):
        for i in range(3):
            send4[pl.ds(2 * i + part, 64, stride=6), :] = value[64 * i : 64 * i + 64]
    exchange(send4, recv4, 6, 4)
    arrived(recv4, 4)
    product = table_times(
        sel_x[...], jnp.concatenate([get_rows(recv4, 0, 1), get_rows(recv4, 1, 1)], 1)
    )
    real, imag = combine_tables(product, FX, FY, 1.0)
    diff_real = focal_real - real
    diff_imag = focal_imag - imag
    window[:FX] = focal_real - (gamma_real * diff_real - gamma_imag * diff_imag)
    window[FX:] = focal_imag - (gamma_real * diff_imag + gamma_imag * diff_real)

    at_home = (mine == s) & (freq % 2 == f % 2)

    def window_copy(target):
        return pltpu.make_async_remote_copy(
            src_ref=window,
            dst_ref=windows.at[freq],
            send_sem=send_sem.at[5],
            recv_sem=pass_sem.at[freq],
            device_id=(target, mine),
            device_id_type=MESH,
        )

    for step in range(4):
        target = 2 * lax.rem(f // 2 + step, 4) + freq % 2
        if step:
            window_copy(target).start()
        else:

            @pl.when(at_home)
            def _():
                pltpu.make_async_copy(window, windows.at[freq], pass_sem.at[freq]).start()

            @pl.when(jnp.logical_not(at_home))
            def _():
                window_copy(target).start()

    def landed(j):
        pltpu.make_async_copy(windows.at[j], windows.at[j], pass_sem.at[j]).wait()

    sibling = f + 1 - 2 * (f % 2)
    for step in range(4):
        j = 2 * lax.rem(f // 2 + step, 4) + f % 2
        landed(j)
        pltpu.make_async_remote_copy(
            src_ref=windows.at[j],
            dst_ref=windows.at[j],
            send_sem=relay_sem,
            recv_sem=pass_sem.at[j],
            device_id=(sibling, s),
            device_id_type=MESH,
        ).start()
    for step in range(4):
        landed(2 * step + 1 - f % 2)
    for t in range(8):
        total = jnp.zeros((FX, FY), F32)
        for j in range(NF):
            phase = (8 * f + t) * (BASE_BIN + j) % TS
            total = total + wave_table[0, phase] * windows[j, :FX] - wave_table[1, phase] * windows[j, FX:]
        out[t, 0] = total

    @pl.when(jnp.logical_not(stays))
    def _():
        pltpu.make_async_copy(labels, labels, send_sem.at[1]).wait()

    sent(send2, 12 * 63, 2)
    sent(send3, 12 * 63, 3)
    sent(send4, 6 * 63, 4)

    @pl.when(at_home)
    def _():
        part = windows.at[pl.ds(0, 3)]
        pltpu.make_async_copy(part, part, send_sem.at[5]).wait()

    @pl.when(jnp.logical_not(at_home))
    def _():
        part = windows.at[pl.ds(0, 4)]
        pltpu.make_async_copy(part, part, send_sem.at[5]).wait()

    relayed = windows.at[pl.ds(0, 4)]
    pltpu.make_async_copy(relayed, relayed, relay_sem).wait()


def solution(mesh):
    table_y, table_x, table_z, wave_table = constant_tables()
    vmem = pl.BlockSpec(memory_space=pltpu.VMEM)
    hbm = pl.BlockSpec(memory_space=pltpu.HBM)
    smem = pl.BlockSpec(memory_space=pltpu.SMEM)

    def local(source, labels, speed_table, atten_table, offsets):
        chunks = pltpu.VMEM((64 * 12, 128), F32)
        small = pltpu.VMEM((64 * 6, 128), F32)
        return pl.pallas_call(
            kernel,
            out_shape=jax.ShapeDtypeStruct((TS // NF, 1, FX, FY), F32),
            in_specs=[hbm, hbm, smem, smem, smem, hbm, hbm, hbm, smem],
            out_specs=vmem,
            scratch_shapes=[
                pltpu.VMEM((2, NX, NY), F32),
                pltpu.VMEM(table_y.shape, BF16),
                pltpu.VMEM(table_x.shape, BF16),
                pltpu.VMEM(table_z.shape, BF16),
                chunks, chunks, chunks, chunks, chunks, chunks, small, small,
                pltpu.VMEM((NX, NY), jnp.int32),
                pltpu.VMEM((2 * FX, FY), F32),
                pltpu.VMEM((NF, 2 * FX, FY), F32),
                pltpu.VMEM((2, NZ, 3 * NY), F32),
                pltpu.VMEM((2, NZ, 3 * NY), F32),
                pltpu.VMEM((2, NX, NY), F32),
                pltpu.VMEM((2 * NY, 2 * FY), BF16),
                pltpu.VMEM((2 * FX, 3 * NX), BF16),
                pltpu.SemaphoreType.DMA((4,)),
                pltpu.SemaphoreType.DMA((6,)),
                pltpu.SemaphoreType.DMA((6,)),
                pltpu.SemaphoreType.DMA((NF,)),
                pltpu.SemaphoreType.DMA,
            ],
            compiler_params=pltpu.CompilerParams(
                collective_id=0, has_side_effects=True, vmem_limit_bytes=63 * 1024 * 1024
            ),
        )(
            source[0, :, 0], labels[0], speed_table, atten_table, offsets,
            jnp.asarray(table_y), jnp.asarray(table_x), jnp.asarray(table_z), jnp.asarray(wave_table),
        )

    return jax.shard_map(
        local,
        mesh=mesh,
        in_specs=(P("freq", None, "slab", None, None), P("slab", None, None), P(), P(), P()),
        out_specs=P("freq", "slab", None, None),
        check_vma=False,
    )
```

```python
import functools
import math

import jax
import jax.numpy as jnp
import numpy as np
from jax import lax
from jax.experimental import pallas as pl
from jax.experimental.pallas import tpu as pltpu
from jax.sharding import PartitionSpec as P

MESH = pl.DeviceIdType.MESH
NX, NY, NZ = 192, 256, 64
FX, FY, NF, TS, NMAT = 32, 128, 8, 64, 8
LABELS, WINDOW = 8, 9
BOTH, EACH = ((0, 12, 2),), ((0, 6, 2), (1, 6, 2))
PARTS1, PARTS2, PARTS3 = BOTH, BOTH, BOTH
HALF = 128
BASE_BIN, K_UNIT = 4, 0.1
F32, BF16 = jnp.float32, jnp.bfloat16


def dft_tables(count):
    points = np.arange(count)
    angle = (points[:, None] * points[None, :] % count) * (2.0 * math.pi / count)
    return np.cos(angle), np.sin(angle)


def halves(table):
    high = np.asarray(table, np.float32).astype(jnp.bfloat16)
    low = (np.asarray(table, np.float64) - high.astype(np.float64)).astype(jnp.bfloat16)
    return high, low


def constant_tables():
    cos_y, sin_y = dft_tables(NY)
    high, low = halves(
        np.concatenate([cos_y[:, :HALF], sin_y[:, :HALF], cos_y[:, HALF:], sin_y[:, HALF:]], 1)
    )
    table_y = np.concatenate([high, high, low], 0)
    cos_x, sin_x = dft_tables(NX)
    high, low = halves(np.concatenate([cos_x, sin_x], 0))
    table_x = np.concatenate([high, high, low], 1)
    cos_z, sin_z = dft_tables(NZ)
    high, low = halves(np.concatenate([cos_z, sin_z], 0))
    table_z = np.concatenate([high, high, low], 1)
    angle = np.arange(TS) * (2.0 * math.pi / TS)
    wave = np.stack([np.cos(angle), np.sin(angle)]).astype(np.float32)
    return table_y, table_x, table_z, wave


def split(value):
    high = value.astype(BF16)
    return high, (value - high.astype(F32)).astype(BF16)


def dot(left, right):
    return jnp.dot(left, right, preferred_element_type=F32)


def times_table(value, table):
    high, low = split(value)
    return dot(jnp.concatenate([high, low, high], 1), table)


def table_times(table, value):
    high, low = split(value)
    return dot(table, jnp.concatenate([high, low, high], 0))


def combine_rows(product, rows, width, sign):
    real = product[:rows, :width] - sign * product[rows:, width:]
    imag = product[rows:, :width] + sign * product[:rows, width:]
    return real, imag


def combine_tables(product, rows, width, sign):
    real = product[:rows, :width] - sign * product[rows:, width:]
    imag = product[:rows, width:] + sign * product[rows:, :width]
    return real, imag


def along_y(real, imag, table, half, sign):
    product = times_table(
        jnp.concatenate([real, imag], 0), table[:, 2 * HALF * half : 2 * HALF * (half + 1)]
    )
    return combine_rows(product, NX, HALF, sign)


def along_x(real, imag, table, sign):
    width = real.shape[1]
    return combine_tables(
        table_times(table, jnp.concatenate([real, imag], 1)), NX, width, sign
    )


def along_z(real, imag, table, sign):
    width = real.shape[1]
    return combine_tables(
        table_times(table, jnp.concatenate([real, imag], 1)), NZ, width, sign
    )


def rows_of(half, i, part, per):
    return pl.ds(6 * half + 2 * i + part, 64, stride=6 * per)


def put_rows(ref, real, imag, half, per=2):
    for part, value in enumerate((real, imag)):
        for i in range(3):
            ref[rows_of(half, i, part, per), :] = value[64 * i : 64 * i + 64]


def get_rows(ref, part, half, per=2):
    return jnp.concatenate([ref[rows_of(half, i, part, per), :] for i in range(3)], 0)


def get_lines(ref, part, half):
    return jnp.concatenate([ref[rows_of(half, i, part, 2), :] for i in range(3)], 1)


def put_lines(ref, real, imag, half):
    for part, value in enumerate((real, imag)):
        for i in range(3):
            ref[rows_of(half, i, part, 2), :] = value[:, HALF * i : HALF * (i + 1)]


def folded_square(index, count):
    folded = jnp.where(index <= count // 2, index, index - count)
    wavenum = folded.astype(F32) * (2.0 * math.pi / count)
    return wavenum * wavenum


def role_device(frequency, k):
    block = frequency // 2 + 4 * (frequency % 2)
    return 4 * (block % 2) + k // 16, 16 * (block // 2) + k % 16


def kernel(
    source_in, labels, speed_in, atten_in, offsets_in, table_y_in, table_x_in, table_z_in, wave_in, out,
    source, table_y, table_x, table_z, speed, atten, offsets, wave_table,
    send1, recv1, send2, recv2, send3, recv3, send4, recv4, tissue, window, windows,
    green, spectrum, field_buf, sel_y, sel_x, load_sem, send_sem, recv_sem, pass_sem, relay_sem, swap_sem,
):
    f = lax.axis_index("freq")
    s = lax.axis_index("slab")
    block = 2 * (s // 16) + f // 4
    freq = 2 * (block % 4) + block // 4
    mine = 16 * (f % 4) + s % 16
    home = freq == f

    loads = [
        pltpu.make_async_copy(src, dst, load_sem.at[i])
        for i, (src, dst) in enumerate(
            (
                (source_in, source), (table_y_in, table_y), (table_x_in, table_x), (table_z_in, table_z),
                (speed_in, speed), (atten_in, atten), (offsets_in, offsets), (wave_in, wave_table),
            )
        )
    ]
    for load in loads:
        load.start()

    barrier = pltpu.get_barrier_semaphore()

    def greet(i, carry):
        pl.semaphore_signal(barrier, inc=1, device_id=(freq, i), device_id_type=MESH)
        return carry

    lax.fori_loop(0, 64, greet, 0)

    for step in range(1, NF):
        near = lax.rem(f + step, NF)
        pl.semaphore_signal(barrier, inc=1, device_id=(near, s), device_id_type=MESH)

    def remote(src, dst, sem, device):
        return pltpu.make_async_remote_copy(
            src_ref=src,
            dst_ref=dst,
            send_sem=send_sem.at[sem],
            recv_sem=recv_sem.at[sem],
            device_id=device,
            device_id_type=MESH,
        )

    def span(k, part):
        first, rows, per = part
        return pl.ds(6 * per * k + 6 * first, rows)

    def exchange(src, dst, part, sem):
        def step(i, carry):
            k = lax.rem(mine + i, 64)
            remote(
                src.at[span(k, part)], dst.at[span(mine, part)], sem, role_device(freq, k)
            ).start()
            return carry

        lax.fori_loop(1, 64, step, 0)
        own = span(mine, part)
        pltpu.make_async_copy(src.at[own], dst.at[own], recv_sem.at[sem]).start()

    def arrived(ref, sem):
        pltpu.make_async_copy(ref, ref, recv_sem.at[sem]).wait()

    def received(ref, parts, half, sem):
        for first, rows, _ in parts:
            if first == half:
                arrived(ref.at[pl.ds(0, 64 * rows)], sem + first)

    def sent(ref, rows, sem):
        part = ref.at[pl.ds(0, rows)]
        pltpu.make_async_copy(part, part, send_sem.at[sem]).wait()

    loads[0].wait()
    loads[1].wait()
    loads[2].wait()
    for half in range(2):
        real, imag = along_y(source[0], source[1], table_y, half, -1.0)
        real, imag = along_x(real, imag, table_x[...], -1.0)
        put_rows(send1, real, imag, half)
    pl.semaphore_wait(barrier, 64 + NF - 1)

    stays = home & (mine == s)
    first_rows = pl.ds(pl.multiple_of(96 * (f // 2 % 2), 8), 96)
    role_rows = pl.ds(pl.multiple_of(96 * (freq // 2 % 2), 8), 96)
    other_rows = pl.ds(pl.multiple_of(96 - 96 * (freq // 2 % 2), 8), 96)

    early = (f // 2 + 4 * (f % 2) < 3)

    @pl.when(early & stays)
    def _():
        pltpu.make_async_copy(labels.at[first_rows], tissue.at[first_rows], recv_sem.at[LABELS]).start()

    @pl.when(early & jnp.logical_not(stays))
    def _():
        remote(labels.at[first_rows], tissue.at[first_rows], LABELS, role_device(f, s)).start()

    for part in PARTS1:

        def scatter(i, carry, part=part):
            k = lax.rem(mine + i, 64)
            remote(
                send1.at[span(k, part)], recv1.at[span(s, part)], part[0], role_device(f, k)
            ).start()
            return carry

        lax.fori_loop(1, 64, scatter, 0)
        own_send, own_recv = send1.at[span(mine, part)], recv1.at[span(s, part)]

        @pl.when(home)
        def _(part=part, own_send=own_send, own_recv=own_recv):
            pltpu.make_async_copy(own_send, own_recv, recv_sem.at[part[0]]).start()

        @pl.when(jnp.logical_not(home))
        def _(part=part, own_send=own_send, own_recv=own_recv):
            remote(own_send, own_recv, part[0], role_device(f, mine)).start()

    for load in loads[3:]:
        load.wait()

    wave = K_UNIT * (BASE_BIN + freq).astype(F32)
    k0sq = wave * wave
    shape = (8, 128)
    pot_real, pot_imag = [], []
    largest = jnp.zeros(shape, F32)
    for m in range(NMAT):
        ratio = jnp.full(shape, wave) / jnp.full(shape, speed[m])
        ratio = ratio * ratio
        damp = jnp.full(shape, atten[m])
        pot_real.append(ratio * (1.0 - damp * damp) - k0sq)
        pot_imag.append(2.0 * ratio * damp)
        largest = jnp.maximum(largest, pot_real[m] * pot_real[m] + pot_imag[m] * pot_imag[m])
    eps = jnp.sqrt(largest) + 0.1 * k0sq
    pot_imag = [value - eps for value in pot_imag]
    eps_row = eps[0:1, 0:1]
    lines = (NZ, HALF)
    z_sq = folded_square(lax.broadcasted_iota(jnp.int32, lines, 0), NZ)
    for half in range(2):
        y_sq = folded_square(lax.broadcasted_iota(jnp.int32, lines, 1) + HALF * half, NY)
        for i in range(3):
            x_sq = folded_square(jnp.full(lines, 64 * i + mine, jnp.int32), NX)
            shifted = z_sq + x_sq + y_sq - k0sq
            denom = shifted * shifted + eps_row * eps_row
            weight = (1.0 / (NX * NY * NZ)) / denom
            green[half, 0, :, HALF * i : HALF * (i + 1)] = shifted * weight
            green[half, 1, :, HALF * i : HALF * (i + 1)] = eps_row * weight

    off_x, off_y = offsets[0], offsets[1]
    pick_y = (
        lax.broadcasted_iota(jnp.int32, (NY, FY), 0)
        == lax.broadcasted_iota(jnp.int32, (NY, FY), 1) + off_y
    ).astype(F32).astype(BF16)
    pick_x = (
        lax.broadcasted_iota(jnp.int32, (FX, NX), 1)
        == lax.broadcasted_iota(jnp.int32, (FX, NX), 0) + off_x
    ).astype(F32).astype(BF16)
    for j, at in enumerate((0, 2 * NY)):
        for part in range(2):
            piece = jnp.concatenate(
                [
                    table_y[at : at + NY, HALF * (2 * half + part) : HALF * (2 * half + part + 1)]
                    for half in range(2)
                ],
                1,
            )
            sel_y[NY * j : NY * (j + 1), FY * part : FY * (part + 1)] = dot(piece, pick_y).astype(BF16)
    for part in range(2):
        piece = table_x[NX * part : NX * (part + 1), :]
        sel_x[FX * part : FX * (part + 1), :] = dot(pick_x, piece).astype(BF16)

    for first, rows, _ in PARTS1:

        @pl.when(home)
        def _(first=first, rows=rows):
            sent(send1, rows * 63, first)

        @pl.when(jnp.logical_not(home))
        def _(first=first, rows=rows):
            sent(send1, rows * 64, first)

    @pl.when(jnp.logical_not(early) & stays)
    def _():
        pltpu.make_async_copy(labels.at[first_rows], tissue.at[first_rows], recv_sem.at[LABELS]).start()

    @pl.when(jnp.logical_not(early) & jnp.logical_not(stays))
    def _():
        remote(labels.at[first_rows], tissue.at[first_rows], LABELS, role_device(f, s)).start()

    def filtered(real, imag, half):
        green_real, green_imag = green[half, 0], green[half, 1]
        return along_z(
            real * green_real - imag * green_imag,
            real * green_imag + imag * green_real,
            table_z[...],
            1.0,
        )

    for half in range(2):
        received(recv1, PARTS1, half, 0)
        real, imag = along_z(
            get_lines(recv1, 0, half), get_lines(recv1, 1, half), table_z[...], -1.0
        )
        spectrum[half, 0] = real
        spectrum[half, 1] = imag
        real, imag = filtered(real, imag, half)
        put_lines(send2, real, imag, half)
        if len(PARTS2) == 2:
            exchange(send2, recv2, PARTS2[half], 2 + half)
    if len(PARTS2) == 1:
        exchange(send2, recv2, PARTS2[0], 2)

    arrived(tissue.at[role_rows], LABELS)
    swap = pltpu.make_async_remote_copy(
        src_ref=tissue.at[role_rows],
        dst_ref=tissue.at[role_rows],
        send_sem=swap_sem.at[0],
        recv_sem=swap_sem.at[1],
        device_id=(f + 4 - 8 * (f // 4), s),
        device_id_type=MESH,
    )
    swap.start()
    pieces = []
    for half in range(2):
        received(recv2, PARTS2, half, 2)
        pieces.append(
            along_x(get_rows(recv2, 0, half), get_rows(recv2, 1, half), table_x[...], 1.0)
        )
    real, imag = (jnp.concatenate(pair, 1) for pair in zip(*pieces, strict=True))
    pieces = [along_y(real, imag, table_y, half, 1.0) for half in range(2)]
    real, imag = (jnp.concatenate(pair, 1) for pair in zip(*pieces, strict=True))
    pltpu.make_async_copy(tissue.at[other_rows], tissue.at[other_rows], swap_sem.at[1]).wait()
    plane = (NX, NY)
    ids = tissue[...]
    cell_real = jnp.zeros(plane, F32)
    cell_imag = jnp.zeros(plane, F32)
    for m in range(NMAT):
        matched = ids == m
        cell_real = jnp.where(matched, pot_real[m][0:1, 0:1], cell_real)
        cell_imag = jnp.where(matched, pot_imag[m][0:1, 0:1], cell_imag)
    inv_eps = 1.0 / eps_row
    gamma_real, gamma_imag = -cell_imag * inv_eps, cell_real * inv_eps
    field_real = gamma_real * real - gamma_imag * imag
    field_imag = gamma_real * imag + gamma_imag * real
    field_buf[0] = field_real
    field_buf[1] = field_imag
    work_real = cell_real * field_real - cell_imag * field_imag
    work_imag = cell_real * field_imag + cell_imag * field_real
    for half in range(2):
        real, imag = along_y(work_real, work_imag, table_y, half, -1.0)
        real, imag = along_x(real, imag, table_x[...], -1.0)
        put_rows(send3, real, imag, half)
        if len(PARTS3) == 2:
            exchange(send3, recv3, PARTS3[half], 4 + half)
    if len(PARTS3) == 1:
        exchange(send3, recv3, PARTS3[0], 4)

    def focal(high_mid_low):
        total = None
        for piece in high_mid_low:
            picked = dot(dot(pick_x, piece).astype(BF16), pick_y)
            total = picked if total is None else total + picked
        return total

    def thirds(value):
        high, rest = split(value)
        low = (value - high.astype(F32) - rest.astype(F32)).astype(BF16)
        return high, rest, low

    focal_ids = focal([tissue[...].astype(F32).astype(BF16)])
    focal_real = focal(thirds(field_buf[0]))
    focal_imag = focal(thirds(field_buf[1]))
    cell_real = jnp.zeros((FX, FY), F32)
    cell_imag = jnp.zeros((FX, FY), F32)
    for m in range(NMAT):
        matched = focal_ids == float(m)
        cell_real = jnp.where(matched, pot_real[m][0:1, 0:1], cell_real)
        cell_imag = jnp.where(matched, pot_imag[m][0:1, 0:1], cell_imag)
    gamma_real, gamma_imag = -cell_imag * inv_eps, cell_real * inv_eps

    product = jnp.zeros((6 * NZ, 2 * FY), F32)
    for half in range(2):
        received(recv3, PARTS3, half, 4)
        real, imag = along_z(
            get_lines(recv3, 0, half), get_lines(recv3, 1, half), table_z[...], -1.0
        )
        real, imag = filtered(real + spectrum[half, 0], imag + spectrum[half, 1], half)
        stacked = jnp.concatenate(
            [value[:, HALF * i : HALF * (i + 1)] for value in (real, imag) for i in range(3)], 0
        )
        high = sel_y[HALF * half : HALF * (half + 1)]
        low = sel_y[NY + HALF * half : NY + HALF * (half + 1)]
        product = product + times_table(stacked, jnp.concatenate([high, high, low], 0))
    real, imag = combine_rows(product, 3 * NZ, FY, 1.0)
    put_rows(send4, real, imag, 0, 1)
    exchange(send4, recv4, (0, 6, 1), 6)
    arrived(recv4, 6)
    product = table_times(
        sel_x[...], jnp.concatenate([get_rows(recv4, 0, 0, 1), get_rows(recv4, 1, 0, 1)], 1)
    )
    real, imag = combine_tables(product, FX, FY, 1.0)
    diff_real = focal_real - real
    diff_imag = focal_imag - imag
    window[:FX] = focal_real - (gamma_real * diff_real - gamma_imag * diff_imag)
    window[FX:] = focal_imag - (gamma_real * diff_imag + gamma_imag * diff_real)

    at_home = (mine == s) & (freq % 2 == f % 2)

    def window_copy(target):
        return pltpu.make_async_remote_copy(
            src_ref=window,
            dst_ref=windows.at[freq],
            send_sem=send_sem.at[WINDOW],
            recv_sem=pass_sem.at[freq],
            device_id=(target, mine),
            device_id_type=MESH,
        )

    for step in range(4):
        target = 2 * lax.rem(f // 2 + step, 4) + freq % 2
        if step:
            window_copy(target).start()
        else:

            @pl.when(at_home)
            def _():
                pltpu.make_async_copy(window, windows.at[freq], pass_sem.at[freq]).start()

            @pl.when(jnp.logical_not(at_home))
            def _():
                window_copy(target).start()

    def landed(j):
        pltpu.make_async_copy(windows.at[j], windows.at[j], pass_sem.at[j]).wait()

    sibling = f + 1 - 2 * (f % 2)
    for step in range(4):
        j = 2 * lax.rem(f // 2 + step, 4) + f % 2
        landed(j)
        pltpu.make_async_remote_copy(
            src_ref=windows.at[j],
            dst_ref=windows.at[j],
            send_sem=relay_sem,
            recv_sem=pass_sem.at[j],
            device_id=(sibling, s),
            device_id_type=MESH,
        ).start()
    for step in range(4):
        landed(2 * step + 1 - f % 2)
    for t in range(8):
        total = jnp.zeros((FX, FY), F32)
        for j in range(NF):
            phase = (8 * f + t) * (BASE_BIN + j) % TS
            total = total + wave_table[0, phase] * windows[j, :FX] - wave_table[1, phase] * windows[j, FX:]
        out[t, 0] = total

    @pl.when(jnp.logical_not(stays))
    def _():
        pltpu.make_async_copy(tissue.at[first_rows], tissue.at[first_rows], send_sem.at[LABELS]).wait()

    swap.wait_send()
    for first, rows, _ in PARTS2:
        sent(send2, rows * 63, 2 + first)
    for first, rows, _ in PARTS3:
        sent(send3, rows * 63, 4 + first)
    sent(send4, 6 * 63, 6)

    @pl.when(at_home)
    def _():
        part = windows.at[pl.ds(0, 3)]
        pltpu.make_async_copy(part, part, send_sem.at[WINDOW]).wait()

    @pl.when(jnp.logical_not(at_home))
    def _():
        part = windows.at[pl.ds(0, 4)]
        pltpu.make_async_copy(part, part, send_sem.at[WINDOW]).wait()

    relayed = windows.at[pl.ds(0, 4)]
    pltpu.make_async_copy(relayed, relayed, relay_sem).wait()


def solution(mesh):
    table_y, table_x, table_z, wave_table = constant_tables()
    vmem = pl.BlockSpec(memory_space=pltpu.VMEM)
    hbm = pl.BlockSpec(memory_space=pltpu.HBM)

    def local(source, labels, speed_table, atten_table, offsets):
        chunks = pltpu.VMEM((64 * 12, 128), F32)
        small = pltpu.VMEM((64 * 6, 128), F32)
        return pl.pallas_call(
            kernel,
            out_shape=jax.ShapeDtypeStruct((TS // NF, 1, FX, FY), F32),
            in_specs=[hbm] * 9,
            out_specs=vmem,
            scratch_shapes=[
                pltpu.VMEM((2, NX, NY), F32),
                pltpu.VMEM(table_y.shape, BF16),
                pltpu.VMEM(table_x.shape, BF16),
                pltpu.VMEM(table_z.shape, BF16),
                pltpu.SMEM((NMAT,), F32),
                pltpu.SMEM((NMAT,), F32),
                pltpu.SMEM((2,), jnp.int32),
                pltpu.SMEM((2, TS), F32),
                chunks, chunks, chunks, chunks, chunks, chunks, small, small,
                pltpu.VMEM((NX, NY), jnp.int32),
                pltpu.VMEM((2 * FX, FY), F32),
                pltpu.VMEM((NF, 2 * FX, FY), F32),
                pltpu.VMEM((2, 2, NZ, 3 * HALF), F32),
                pltpu.VMEM((2, 2, NZ, 3 * HALF), F32),
                pltpu.VMEM((2, NX, NY), F32),
                pltpu.VMEM((2 * NY, 2 * FY), BF16),
                pltpu.VMEM((2 * FX, 3 * NX), BF16),
                pltpu.SemaphoreType.DMA((8,)),
                pltpu.SemaphoreType.DMA((10,)),
                pltpu.SemaphoreType.DMA((10,)),
                pltpu.SemaphoreType.DMA((NF,)),
                pltpu.SemaphoreType.DMA,
                pltpu.SemaphoreType.DMA((2,)),
            ],
            compiler_params=pltpu.CompilerParams(
                collective_id=0, has_side_effects=True, vmem_limit_bytes=63 * 1024 * 1024
            ),
        )(
            source[0, :, 0], labels[0], speed_table, atten_table, offsets,
            jnp.asarray(table_y), jnp.asarray(table_x), jnp.asarray(table_z), jnp.asarray(wave_table),
        )

    return jax.shard_map(
        local,
        mesh=mesh,
        in_specs=(P("freq", None, "slab", None, None), P("slab", None, None), P(), P(), P()),
        out_specs=P("freq", "slab", None, None),
        check_vma=False,
    )
```

```python
import functools
import math

import jax
import jax.numpy as jnp
import numpy as np
from jax import lax
from jax.experimental import pallas as pl
from jax.experimental.pallas import tpu as pltpu
from jax.sharding import PartitionSpec as P

MESH = pl.DeviceIdType.MESH
NX, NY, NZ = 192, 256, 64
FX, FY, NF, TS, NMAT = 32, 128, 8, 64, 8
LABELS, WINDOW = 8, 9
BOTH, EACH = ((0, 12, 2),), ((0, 6, 2), (1, 6, 2))
PARTS1, PARTS2, PARTS3 = BOTH, BOTH, BOTH
HALF = 128
BASE_BIN, K_UNIT = 4, 0.1
F32, BF16 = jnp.float32, jnp.bfloat16


def dft_tables(count):
    points = np.arange(count)
    angle = (points[:, None] * points[None, :] % count) * (2.0 * math.pi / count)
    return np.cos(angle), np.sin(angle)


def halves(table):
    high = np.asarray(table, np.float32).astype(jnp.bfloat16)
    low = (np.asarray(table, np.float64) - high.astype(np.float64)).astype(jnp.bfloat16)
    return high, low


def constant_tables():
    cos_y, sin_y = dft_tables(NY)
    high, low = halves(
        np.concatenate([cos_y[:, :HALF], sin_y[:, :HALF], cos_y[:, HALF:], sin_y[:, HALF:]], 1)
    )
    table_y = np.concatenate([high, high, low], 0)
    cos_x, sin_x = dft_tables(NX)
    high, low = halves(np.concatenate([cos_x, sin_x], 0))
    table_x = np.concatenate([high, high, low], 1)
    cos_z, sin_z = dft_tables(NZ)
    high, low = halves(np.concatenate([cos_z, sin_z], 0))
    table_z = np.concatenate([high, high, low], 1)
    angle = np.arange(TS) * (2.0 * math.pi / TS)
    wave = np.stack([np.cos(angle), np.sin(angle)]).astype(np.float32)
    return table_y, table_x, table_z, wave


def split(value):
    high = value.astype(BF16)
    return high, (value - high.astype(F32)).astype(BF16)


def dot(left, right):
    return jnp.dot(left, right, preferred_element_type=F32)


def times_table(value, table):
    high, low = split(value)
    return dot(jnp.concatenate([high, low, high], 1), table)


def table_times(table, value):
    high, low = split(value)
    return dot(table, jnp.concatenate([high, low, high], 0))


def combine_rows(product, rows, width, sign):
    real = product[:rows, :width] - sign * product[rows:, width:]
    imag = product[rows:, :width] + sign * product[:rows, width:]
    return real, imag


def combine_tables(product, rows, width, sign):
    real = product[:rows, :width] - sign * product[rows:, width:]
    imag = product[:rows, width:] + sign * product[rows:, :width]
    return real, imag


def along_y(real, imag, table, half, sign):
    product = times_table(
        jnp.concatenate([real, imag], 0), table[:, 2 * HALF * half : 2 * HALF * (half + 1)]
    )
    return combine_rows(product, NX, HALF, sign)


def along_x(real, imag, table, sign):
    width = real.shape[1]
    return combine_tables(
        table_times(table, jnp.concatenate([real, imag], 1)), NX, width, sign
    )


def along_z(real, imag, table, sign):
    width = real.shape[1]
    return combine_tables(
        table_times(table, jnp.concatenate([real, imag], 1)), NZ, width, sign
    )


def rows_of(half, i, part, per):
    return pl.ds(6 * half + 2 * i + part, 64, stride=6 * per)


def put_rows(ref, real, imag, half, per=2):
    for part, value in enumerate((real, imag)):
        for i in range(3):
            ref[rows_of(half, i, part, per), :] = value[64 * i : 64 * i + 64]


def get_rows(ref, part, half, per=2):
    return jnp.concatenate([ref[rows_of(half, i, part, per), :] for i in range(3)], 0)


def get_lines(ref, part, half):
    return jnp.concatenate([ref[rows_of(half, i, part, 2), :] for i in range(3)], 1)


def put_lines(ref, real, imag, half):
    for part, value in enumerate((real, imag)):
        for i in range(3):
            ref[rows_of(half, i, part, 2), :] = value[:, HALF * i : HALF * (i + 1)]


def folded_square(index, count):
    folded = jnp.where(index <= count // 2, index, index - count)
    wavenum = folded.astype(F32) * (2.0 * math.pi / count)
    return wavenum * wavenum


def role_device(frequency, k):
    block = frequency // 2 + 4 * (frequency % 2)
    return 4 * (block % 2) + k // 16, 16 * (block // 2) + k % 16


def kernel(
    source_in, labels, speed_in, atten_in, offsets_in, table_y_in, table_x_in, table_z_in, wave_in, out,
    source, table_y, table_x, table_z, speed, atten, offsets, wave_table,
    send1, recv1, send2, recv2, send3, recv3, send4, recv4, tissue, window, windows,
    green, spectrum, field_buf, sel_y, sel_x, load_sem, send_sem, recv_sem, pass_sem, relay_sem, swap_sem,
):
    f = lax.axis_index("freq")
    s = lax.axis_index("slab")
    block = 2 * (s // 16) + f // 4
    freq = 2 * (block % 4) + block // 4
    mine = 16 * (f % 4) + s % 16
    home = freq == f

    loads = [
        pltpu.make_async_copy(src, dst, load_sem.at[i])
        for i, (src, dst) in enumerate(
            (
                (source_in, source), (table_y_in, table_y), (table_x_in, table_x), (table_z_in, table_z),
                (speed_in, speed), (atten_in, atten), (offsets_in, offsets), (wave_in, wave_table),
            )
        )
    ]
    for load in loads:
        load.start()

    barrier = pltpu.get_barrier_semaphore()

    def greet(i, carry):
        pl.semaphore_signal(barrier, inc=1, device_id=(freq, i), device_id_type=MESH)
        return carry

    lax.fori_loop(0, 64, greet, 0)

    for step in range(1, NF):
        near = lax.rem(f + step, NF)
        pl.semaphore_signal(barrier, inc=1, device_id=(near, s), device_id_type=MESH)

    def remote(src, dst, sem, device):
        return pltpu.make_async_remote_copy(
            src_ref=src,
            dst_ref=dst,
            send_sem=send_sem.at[sem],
            recv_sem=recv_sem.at[sem],
            device_id=device,
            device_id_type=MESH,
        )

    def span(k, part):
        first, rows, per = part
        return pl.ds(6 * per * k + 6 * first, rows)

    def exchange(src, dst, part, sem):
        def step(i, carry):
            k = lax.rem(mine + i, 64)
            remote(
                src.at[span(k, part)], dst.at[span(mine, part)], sem, role_device(freq, k)
            ).start()
            return carry

        lax.fori_loop(1, 64, step, 0)
        own = span(mine, part)
        pltpu.make_async_copy(src.at[own], dst.at[own], recv_sem.at[sem]).start()

    def arrived(ref, sem):
        pltpu.make_async_copy(ref, ref, recv_sem.at[sem]).wait()

    def received(ref, parts, half, sem):
        for first, rows, _ in parts:
            if first == half:
                arrived(ref.at[pl.ds(0, 64 * rows)], sem + first)

    def sent(ref, rows, sem):
        part = ref.at[pl.ds(0, rows)]
        pltpu.make_async_copy(part, part, send_sem.at[sem]).wait()

    loads[0].wait()
    loads[1].wait()
    loads[2].wait()
    for half in range(2):
        real, imag = along_y(source[0], source[1], table_y, half, -1.0)
        real, imag = along_x(real, imag, table_x[...], -1.0)
        put_rows(send1, real, imag, half)
    pl.semaphore_wait(barrier, 64 + NF - 1)

    stays = home & (mine == s)
    first_rows = pl.ds(pl.multiple_of(96 * (f // 2 % 2), 8), 96)
    role_rows = pl.ds(pl.multiple_of(96 * (freq // 2 % 2), 8), 96)
    other_rows = pl.ds(pl.multiple_of(96 - 96 * (freq // 2 % 2), 8), 96)

    early = (f // 2 + 4 * (f % 2) < 3)

    @pl.when(early & stays)
    def _():
        pltpu.make_async_copy(labels.at[first_rows], tissue.at[first_rows], recv_sem.at[LABELS]).start()

    @pl.when(early & jnp.logical_not(stays))
    def _():
        remote(labels.at[first_rows], tissue.at[first_rows], LABELS, role_device(f, s)).start()

    for part in PARTS1:

        def scatter(i, carry, part=part):
            k = lax.rem(mine + i, 64)
            remote(
                send1.at[span(k, part)], recv1.at[span(s, part)], part[0], role_device(f, k)
            ).start()
            return carry

        lax.fori_loop(1, 64, scatter, 0)
        own_send, own_recv = send1.at[span(mine, part)], recv1.at[span(s, part)]

        @pl.when(home)
        def _(part=part, own_send=own_send, own_recv=own_recv):
            pltpu.make_async_copy(own_send, own_recv, recv_sem.at[part[0]]).start()

        @pl.when(jnp.logical_not(home))
        def _(part=part, own_send=own_send, own_recv=own_recv):
            remote(own_send, own_recv, part[0], role_device(f, mine)).start()

    for load in loads[3:]:
        load.wait()

    wave = K_UNIT * (BASE_BIN + freq).astype(F32)
    k0sq = wave * wave
    shape = (8, 128)
    pot_real, pot_imag = [], []
    largest = jnp.zeros(shape, F32)
    for m in range(NMAT):
        ratio = jnp.full(shape, wave) / jnp.full(shape, speed[m])
        ratio = ratio * ratio
        damp = jnp.full(shape, atten[m])
        pot_real.append(ratio * (1.0 - damp * damp) - k0sq)
        pot_imag.append(2.0 * ratio * damp)
        largest = jnp.maximum(largest, pot_real[m] * pot_real[m] + pot_imag[m] * pot_imag[m])
    eps = jnp.sqrt(largest) + 0.1 * k0sq
    pot_imag = [value - eps for value in pot_imag]
    eps_row = eps[0:1, 0:1]
    lines = (NZ, HALF)
    z_sq = folded_square(lax.broadcasted_iota(jnp.int32, lines, 0), NZ)
    for half in range(2):
        y_sq = folded_square(lax.broadcasted_iota(jnp.int32, lines, 1) + HALF * half, NY)
        for i in range(3):
            x_sq = folded_square(jnp.full(lines, 64 * i + mine, jnp.int32), NX)
            shifted = z_sq + x_sq + y_sq - k0sq
            denom = shifted * shifted + eps_row * eps_row
            weight = (1.0 / (NX * NY * NZ)) / denom
            green[half, 0, :, HALF * i : HALF * (i + 1)] = shifted * weight
            green[half, 1, :, HALF * i : HALF * (i + 1)] = eps_row * weight

    off_x, off_y = offsets[0], offsets[1]
    pick_y = (
        lax.broadcasted_iota(jnp.int32, (NY, FY), 0)
        == lax.broadcasted_iota(jnp.int32, (NY, FY), 1) + off_y
    ).astype(F32).astype(BF16)
    pick_x = (
        lax.broadcasted_iota(jnp.int32, (FX, NX), 1)
        == lax.broadcasted_iota(jnp.int32, (FX, NX), 0) + off_x
    ).astype(F32).astype(BF16)
    for j, at in enumerate((0, 2 * NY)):
        for part in range(2):
            piece = jnp.concatenate(
                [
                    table_y[at : at + NY, HALF * (2 * half + part) : HALF * (2 * half + part + 1)]
                    for half in range(2)
                ],
                1,
            )
            sel_y[NY * j : NY * (j + 1), FY * part : FY * (part + 1)] = dot(piece, pick_y).astype(BF16)
    for part in range(2):
        piece = table_x[NX * part : NX * (part + 1), :]
        sel_x[FX * part : FX * (part + 1), :] = dot(pick_x, piece).astype(BF16)

    for first, rows, _ in PARTS1:

        @pl.when(home)
        def _(first=first, rows=rows):
            sent(send1, rows * 63, first)

        @pl.when(jnp.logical_not(home))
        def _(first=first, rows=rows):
            sent(send1, rows * 64, first)

    @pl.when(jnp.logical_not(early) & stays)
    def _():
        pltpu.make_async_copy(labels.at[first_rows], tissue.at[first_rows], recv_sem.at[LABELS]).start()

    @pl.when(jnp.logical_not(early) & jnp.logical_not(stays))
    def _():
        remote(labels.at[first_rows], tissue.at[first_rows], LABELS, role_device(f, s)).start()

    def filtered(real, imag, half):
        green_real, green_imag = green[half, 0], green[half, 1]
        return along_z(
            real * green_real - imag * green_imag,
            real * green_imag + imag * green_real,
            table_z[...],
            1.0,
        )

    for half in range(2):
        received(recv1, PARTS1, half, 0)
        real, imag = along_z(
            get_lines(recv1, 0, half), get_lines(recv1, 1, half), table_z[...], -1.0
        )
        spectrum[half, 0] = real
        spectrum[half, 1] = imag
        real, imag = filtered(real, imag, half)
        put_lines(send2, real, imag, half)
        if len(PARTS2) == 2:
            exchange(send2, recv2, PARTS2[half], 2 + half)
    if len(PARTS2) == 1:
        exchange(send2, recv2, PARTS2[0], 2)

    arrived(tissue.at[role_rows], LABELS)
    swap = pltpu.make_async_remote_copy(
        src_ref=tissue.at[role_rows],
        dst_ref=tissue.at[role_rows],
        send_sem=swap_sem.at[0],
        recv_sem=swap_sem.at[1],
        device_id=(f + 4 - 8 * (f // 4), s),
        device_id_type=MESH,
    )
    swap.start()
    pieces = []
    for half in range(2):
        received(recv2, PARTS2, half, 2)
        pieces.append(
            along_x(get_rows(recv2, 0, half), get_rows(recv2, 1, half), table_x[...], 1.0)
        )
    real, imag = (jnp.concatenate(pair, 1) for pair in zip(*pieces, strict=True))
    pieces = [along_y(real, imag, table_y, half, 1.0) for half in range(2)]
    real, imag = (jnp.concatenate(pair, 1) for pair in zip(*pieces, strict=True))
    pltpu.make_async_copy(tissue.at[other_rows], tissue.at[other_rows], swap_sem.at[1]).wait()
    plane = (NX, NY)
    ids = tissue[...]
    cell_real = jnp.zeros(plane, F32)
    cell_imag = jnp.zeros(plane, F32)
    for m in range(NMAT):
        matched = ids == m
        cell_real = jnp.where(matched, pot_real[m][0:1, 0:1], cell_real)
        cell_imag = jnp.where(matched, pot_imag[m][0:1, 0:1], cell_imag)
    inv_eps = 1.0 / eps_row
    gamma_real, gamma_imag = -cell_imag * inv_eps, cell_real * inv_eps
    field_real = gamma_real * real - gamma_imag * imag
    field_imag = gamma_real * imag + gamma_imag * real
    field_buf[0] = field_real
    field_buf[1] = field_imag
    work_real = cell_real * field_real - cell_imag * field_imag
    work_imag = cell_real * field_imag + cell_imag * field_real
    for half in range(2):
        real, imag = along_y(work_real, work_imag, table_y, half, -1.0)
        real, imag = along_x(real, imag, table_x[...], -1.0)
        put_rows(send3, real, imag, half)
        if len(PARTS3) == 2:
            exchange(send3, recv3, PARTS3[half], 4 + half)
    if len(PARTS3) == 1:
        exchange(send3, recv3, PARTS3[0], 4)

    def focal(high_mid_low):
        total = None
        for piece in high_mid_low:
            picked = dot(dot(pick_x, piece).astype(BF16), pick_y)
            total = picked if total is None else total + picked
        return total

    def thirds(value):
        high, rest = split(value)
        low = (value - high.astype(F32) - rest.astype(F32)).astype(BF16)
        return high, rest, low

    focal_ids = focal([tissue[...].astype(F32).astype(BF16)])
    focal_real = focal(thirds(field_buf[0]))
    focal_imag = focal(thirds(field_buf[1]))
    cell_real = jnp.zeros((FX, FY), F32)
    cell_imag = jnp.zeros((FX, FY), F32)
    for m in range(NMAT):
        matched = focal_ids == float(m)
        cell_real = jnp.where(matched, pot_real[m][0:1, 0:1], cell_real)
        cell_imag = jnp.where(matched, pot_imag[m][0:1, 0:1], cell_imag)
    gamma_real, gamma_imag = -cell_imag * inv_eps, cell_real * inv_eps

    product = jnp.zeros((6 * NZ, 2 * FY), F32)
    for half in range(2):
        received(recv3, PARTS3, half, 4)
        real, imag = along_z(
            get_lines(recv3, 0, half), get_lines(recv3, 1, half), table_z[...], -1.0
        )
        real, imag = filtered(real + spectrum[half, 0], imag + spectrum[half, 1], half)
        stacked = jnp.concatenate(
            [value[:, HALF * i : HALF * (i + 1)] for value in (real, imag) for i in range(3)], 0
        )
        high = sel_y[HALF * half : HALF * (half + 1)]
        low = sel_y[NY + HALF * half : NY + HALF * (half + 1)]
        product = product + times_table(stacked, jnp.concatenate([high, high, low], 0))
    real, imag = combine_rows(product, 3 * NZ, FY, 1.0)
    put_rows(send4, real, imag, 0, 1)
    exchange(send4, recv4, (0, 6, 1), 6)
    arrived(recv4.at[pl.ds(0, 64 * 6)], 6)
    product = table_times(
        sel_x[...], jnp.concatenate([get_rows(recv4, 0, 0, 1), get_rows(recv4, 1, 0, 1)], 1)
    )
    real, imag = combine_tables(product, FX, FY, 1.0)
    diff_real = focal_real - real
    diff_imag = focal_imag - imag
    window[:FX] = focal_real - (gamma_real * diff_real - gamma_imag * diff_imag)
    window[FX:] = focal_imag - (gamma_real * diff_imag + gamma_imag * diff_real)

    at_home = (mine == s) & (freq % 2 == f % 2)

    def window_copy(target):
        return pltpu.make_async_remote_copy(
            src_ref=window,
            dst_ref=windows.at[freq],
            send_sem=send_sem.at[WINDOW],
            recv_sem=pass_sem.at[freq],
            device_id=(target, mine),
            device_id_type=MESH,
        )

    for step in range(4):
        target = 2 * lax.rem(f // 2 + step, 4) + freq % 2
        if step:
            window_copy(target).start()
        else:

            @pl.when(at_home)
            def _():
                pltpu.make_async_copy(window, windows.at[freq], pass_sem.at[freq]).start()

            @pl.when(jnp.logical_not(at_home))
            def _():
                window_copy(target).start()

    def landed(j):
        pltpu.make_async_copy(windows.at[j], windows.at[j], pass_sem.at[j]).wait()

    sibling = f + 1 - 2 * (f % 2)
    for step in range(4):
        j = 2 * lax.rem(f // 2 + step, 4) + f % 2
        landed(j)
        pltpu.make_async_remote_copy(
            src_ref=windows.at[j],
            dst_ref=windows.at[j],
            send_sem=relay_sem,
            recv_sem=pass_sem.at[j],
            device_id=(sibling, s),
            device_id_type=MESH,
        ).start()
    for step in range(4):
        landed(2 * step + 1 - f % 2)
    for t in range(8):
        total = jnp.zeros((FX, FY), F32)
        for j in range(NF):
            phase = (8 * f + t) * (BASE_BIN + j) % TS
            total = total + wave_table[0, phase] * windows[j, :FX] - wave_table[1, phase] * windows[j, FX:]
        out[t, 0] = total

    @pl.when(jnp.logical_not(stays))
    def _():
        pltpu.make_async_copy(tissue.at[first_rows], tissue.at[first_rows], send_sem.at[LABELS]).wait()

    swap.wait_send()
    for first, rows, _ in PARTS2:
        sent(send2, rows * 63, 2 + first)
    for first, rows, _ in PARTS3:
        sent(send3, rows * 63, 4 + first)
    sent(send4, 6 * 63, 6)

    @pl.when(at_home)
    def _():
        part = windows.at[pl.ds(0, 3)]
        pltpu.make_async_copy(part, part, send_sem.at[WINDOW]).wait()

    @pl.when(jnp.logical_not(at_home))
    def _():
        part = windows.at[pl.ds(0, 4)]
        pltpu.make_async_copy(part, part, send_sem.at[WINDOW]).wait()

    relayed = windows.at[pl.ds(0, 4)]
    pltpu.make_async_copy(relayed, relayed, relay_sem).wait()


def solution(mesh):
    table_y, table_x, table_z, wave_table = constant_tables()
    vmem = pl.BlockSpec(memory_space=pltpu.VMEM)
    hbm = pl.BlockSpec(memory_space=pltpu.HBM)

    def local(source, labels, speed_table, atten_table, offsets):
        chunks = pltpu.VMEM((64 * 12 + 16, 128), F32)
        small = pltpu.VMEM((64 * 6 + 8, 128), F32)
        return pl.pallas_call(
            kernel,
            out_shape=jax.ShapeDtypeStruct((TS // NF, 1, FX, FY), F32),
            in_specs=[hbm] * 9,
            out_specs=vmem,
            scratch_shapes=[
                pltpu.VMEM((2, NX, NY), F32),
                pltpu.VMEM(table_y.shape, BF16),
                pltpu.VMEM(table_x.shape, BF16),
                pltpu.VMEM(table_z.shape, BF16),
                pltpu.SMEM((NMAT,), F32),
                pltpu.SMEM((NMAT,), F32),
                pltpu.SMEM((2,), jnp.int32),
                pltpu.SMEM((2, TS), F32),
                chunks, chunks, chunks, chunks, chunks, chunks, small, small,
                pltpu.VMEM((NX, NY), jnp.int32),
                pltpu.VMEM((2 * FX, FY), F32),
                pltpu.VMEM((NF, 2 * FX, FY), F32),
                pltpu.VMEM((2, 2, NZ, 3 * HALF), F32),
                pltpu.VMEM((2, 2, NZ, 3 * HALF), F32),
                pltpu.VMEM((2, NX, NY), F32),
                pltpu.VMEM((2 * NY, 2 * FY), BF16),
                pltpu.VMEM((2 * FX, 3 * NX), BF16),
                pltpu.SemaphoreType.DMA((8,)),
                pltpu.SemaphoreType.DMA((10,)),
                pltpu.SemaphoreType.DMA((10,)),
                pltpu.SemaphoreType.DMA((NF,)),
                pltpu.SemaphoreType.DMA,
                pltpu.SemaphoreType.DMA((2,)),
            ],
            compiler_params=pltpu.CompilerParams(
                collective_id=0, has_side_effects=True, vmem_limit_bytes=63 * 1024 * 1024
            ),
        )(
            source[0, :, 0], labels[0], speed_table, atten_table, offsets,
            jnp.asarray(table_y), jnp.asarray(table_x), jnp.asarray(table_z), jnp.asarray(wave_table),
        )

    return jax.shard_map(
        local,
        mesh=mesh,
        in_specs=(P("freq", None, "slab", None, None), P("slab", None, None), P(), P(), P()),
        out_specs=P("freq", "slab", None, None),
        check_vma=False,
    )
```
